128 devices in a mesh: curve: 128 (over x, y, z, core).
Axes of the slice: x: 4, y: 4, z: 4, core: 2. Of those that a mesh axis runs over, the one named last changes fastest.
Arguments:
- history: float32 [1048576, 512], P('curve'), may hold values from -3 to 3
- child_octant: int32 [1048576], P('curve'), may hold values from 0 to 7, as said below
- partition_offsets: int32 [129], replicated, may hold values from 0 to 524288, as said below
- connectivity: int32 [8, 65536], P(None, 'curve'), may hold values from 0 to 1023
- ghost_list: int32 [2, 16384], P(None, 'curve'), may hold values from 0 to 767, as said below
- grain_id: int32 [65536], P('curve'), may hold values from 0 to 63
- schmid: float32 [64, 288], replicated, may hold values from -3 to 3
- displacement: float32 [3, 98304], P(None, 'curve'), may hold values from -3 to 3
- step_size: float32 [98304], P('curve'), may hold values from 0.05 to 0.2
- load: float32 [3, 98304], P(None, 'curve'), may hold values from -3 to 3
Outputs:
- parent_history: float32 [65536, 512], P('curve')
- residual: float32 [3, 98304], P(None, 'curve')
The draws below stay inside these ranges and needn't reach their ends.
Inputs may be any that keep to these rules, and one draw needn't show every extreme that they name: `partition_offsets`: entries never fall; entry 0 is 0 and the last is 524288; entry d lies within 2048 of 8 * 512 * d, and both ends of that band are reached. `child_octant`: the eight children of a parent fill eight different octants. `ghost_list`: the 256 entries of one device are different nodes.
All inputs are finite; a program needn't handle non-finite values.
Results may differ from the reference program's by a relative error of at most 0.0003.
Values sent between devices are 32-bit elements; how exact they have to be, the bound alone decides.
No kernel may reach another device: no remote copies, remote signals or barrier semaphores. Data moves between devices by JAX's collectives and lax.ppermute only.
A program may use at most 192 MiB of HBM per device.

```python
import math
import jax
import jax.numpy as jnp
import numpy as np
from jax import lax

SLIP = 48
HIST = 64
PAR_DEV = 512
GHOST = 128
GRAINS = 64
CH_CAP = 8192
CHILDREN = 524288
PARENTS = 65536
NODE_DEV = 768
NODES = 98304
N_CURVE = 128


def band_offsets(key):
    base_key = jax.random.fold_in(key, 101)
    subkeys = jax.random.split(base_key, 3)
    band_reach = 4 * PAR_DEV
    devices = jnp.arange(N_CURVE + 1)
    shifts = jax.random.randint(subkeys[0], (N_CURVE + 1,), -band_reach, band_reach + 1)
    lowest = jax.random.randint(subkeys[1], (), 1, N_CURVE)
    highest = 1 + (lowest - 1 + jax.random.randint(subkeys[2], (), 1, N_CURVE - 1)) % (N_CURVE - 1)
    shifts = jnp.where(devices == lowest, -band_reach, shifts)
    shifts = jnp.where(devices == highest, band_reach, shifts)
    shifts = jnp.where((devices == 0) | (devices == N_CURVE), 0, shifts)
    return (devices * 8 * PAR_DEV + shifts).astype(jnp.int32)


def draw_partition_offsets(key, part):
    offsets = band_offsets(key)
    return offsets


def draw_child_octant(key, part):
    offsets = band_offsets(key)
    key = jax.random.fold_in(key, 2)
    subkeys = jax.random.split(key, 2)
    scores = jax.random.randint(subkeys[0], (PARENTS, 8), 0, 1 << 20) * 8 + jnp.arange(8)
    sibling_order = jnp.argsort(scores, axis=1, stable=True).astype(jnp.int32).reshape(CHILDREN)
    capacity = 16 * PAR_DEV
    rows_all = jnp.arange(N_CURVE * capacity)
    holder = rows_all // capacity
    child_index = offsets[holder] + rows_all % capacity
    present = child_index < offsets[holder + 1]
    filler = jax.random.randint(subkeys[1], (N_CURVE * capacity,), 0, 8)
    chosen = sibling_order[jnp.clip(child_index, 0, CHILDREN - 1)]
    return jnp.where(present, chosen, filler).astype(jnp.int32)


def draw_ghost_list(key, part):
    key = jax.random.fold_in(key, 3)
    node_keys = jax.random.split(key, N_CURVE)

    def shuffle_nodes(one_key):
        return jax.random.permutation(one_key, PAR_DEV + 2 * GHOST)
    shuffled = jax.vmap(shuffle_nodes)(node_keys)
    chosen = shuffled[:, :2 * GHOST].reshape(N_CURVE, 2, GHOST)
    return jnp.transpose(chosen, (1, 0, 2)).reshape(2, N_CURVE * GHOST).astype(jnp.int32)


def plant(drawn, own_key, least, largest):
    spot = [jax.random.randint(jax.random.fold_in(own_key, axis), (), 0, length) for axis, length in enumerate(drawn.shape)]
    main_axis = drawn.shape.index(max(drawn.shape))
    next_to = spot[:main_axis] + [(spot[main_axis] + 1) % drawn.shape[main_axis]] + spot[main_axis + 1:]
    return drawn.at[tuple(spot)].set(least).at[tuple(next_to)].set(largest)


def levels(own_key, dims, cuts, least, top_value):
    gain, own = 1.0, jax.random.fold_in(own_key, 6)
    for dim, parts in cuts:
        heights = jnp.exp(jax.random.uniform(jax.random.fold_in(own, dim), (parts,), jnp.float32, least / len(cuts), top_value / len(cuts)))
        gain = gain * jnp.repeat(heights, dims[dim] // parts).reshape([-1 if axis == dim else 1 for axis in range(len(dims))])
    return gain


def bell_draw(stream_key, dims, spread, reach, cuts=(), kind=jnp.bfloat16):
    gain = levels(stream_key, dims, cuts, -0.22, 0.18) if cuts else 1.0
    array = jax.random.normal(stream_key, dims, jnp.float32) * spread * gain
    return jnp.minimum(jnp.maximum(array, -reach), reach).astype(kind)


def setup_inputs(seed: int = 0) -> dict:
    splits = jax.random.split(jax.random.key(seed), 11)
    history = bell_draw(splits[0], (CH_CAP * N_CURVE, 8 * HIST), 0.5, 3.0, ((0, 128),), jnp.float32)
    child_octant = draw_child_octant(jax.random.fold_in(splits[10], 71), 0)
    partition_offsets = draw_partition_offsets(jax.random.fold_in(splits[10], 71), 0)
    connectivity = plant(jax.random.randint(splits[3], (8, PARENTS), 0, NODE_DEV + 2 * GHOST), jax.random.fold_in(splits[3], 1), 0, (NODE_DEV + 2 * GHOST) - 1).astype(jnp.int32)
    ghost_list = draw_ghost_list(jax.random.fold_in(splits[10], 71), 0)
    grain_id = plant(jax.random.randint(splits[5], (PARENTS,), 0, GRAINS), jax.random.fold_in(splits[5], 1), 0, GRAINS - 1).astype(jnp.int32)
    schmid = bell_draw(splits[6], (GRAINS, 6 * SLIP), 0.5, 3.0, (), jnp.float32)
    displacement = bell_draw(splits[7], (3, NODES), 0.5, 3.0, ((1, 128),), jnp.float32)
    step_size = jnp.clip(jnp.exp(math.log(0.2) - 1.3862944 * jax.random.uniform(splits[8], (NODES,), jnp.float32) ** levels(splits[8], (NODES,), ((0, 128),), -0.2, 0.2)), 0.05, 0.2)
    load = bell_draw(splits[9], (3, NODES), 0.5, 3.0, ((1, 128),), jnp.float32)
    return dict(history=history, child_octant=child_octant, partition_offsets=partition_offsets, connectivity=connectivity, ghost_list=ghost_list, grain_id=grain_id, schmid=schmid, displacement=displacement, step_size=step_size, load=load)


lame_first = 1.0
shear_modulus = 0.75
slip_rate = 0.1
quad_weight = 0.125

def projection_table():
    root_third = 1.0 / math.sqrt(3.0)
    table = np.zeros((8, 64))
    for target in range(8):
        for octant in range(8):
            for source in range(8):
                weight = 1.0
                for direction in range(3):
                    target_bit = target >> direction & 1
                    octant_bit = octant >> direction & 1
                    source_bit = source >> direction & 1
                    location = octant_bit - 0.5 + (2 * source_bit - 1) * 0.5 * root_third
                    weight = weight * (0.25 + 0.75 * (2 * target_bit - 1) * root_third * location)
                table[target, octant * 8 + source] = weight
    return table

def strain_table():
    root_third = 1.0 / math.sqrt(3.0)
    table = np.zeros((48, 24))
    for quad_point in range(8):
        gauss_points = [(2 * (quad_point >> direction & 1) - 1) * root_third for direction in range(3)]
        for corner in range(8):
            corner_signs = [2 * (corner >> direction & 1) - 1 for direction in range(3)]
            slopes = []
            for direction in range(3):
                factor = 0.25 * corner_signs[direction]
                for other_axis in range(3):
                    if other_axis != direction:
                        factor = factor * (1.0 + corner_signs[other_axis] * gauss_points[other_axis])
                slopes.append(factor)
            row_base = quad_point * 6
            table[row_base + 0, corner] += slopes[0]
            table[row_base + 1, 8 + corner] += slopes[1]
            table[row_base + 2, 16 + corner] += slopes[2]
            table[row_base + 3, 8 + corner] += slopes[2]
            table[row_base + 3, 16 + corner] += slopes[1]
            table[row_base + 4, corner] += slopes[2]
            table[row_base + 4, 16 + corner] += slopes[0]
            table[row_base + 5, corner] += slopes[1]
            table[row_base + 5, 8 + corner] += slopes[0]
    return table

def elastic(strains):
    volume = strains[:, 0] + strains[:, 1] + strains[:, 2]
    normal = lame_first * volume[:, None] + 2.0 * shear_modulus * strains[:, :3]
    return jnp.concatenate([normal, shear_modulus * strains[:, 3:]], axis=1)

def forces(corner_values, history_points, schmid_points):
    element_count = corner_values.shape[-1]
    derivative = jnp.asarray(strain_table(), jnp.float32)
    strain = jnp.dot(derivative, corner_values.reshape(24, element_count), precision=lax.Precision.HIGHEST)
    strain = strain.reshape(8, 6, element_count)
    slip_log = history_points[:, :SLIP]
    plastic = history_points[:, SLIP:SLIP + 6]
    trial_stress = elastic(strain - plastic)
    resolved = jnp.einsum('qkp,kap->qap', trial_stress, schmid_points, precision=lax.Precision.HIGHEST)
    slip_amount = slip_rate * jnp.tanh(resolved * jnp.exp(-slip_log))
    increment = jnp.einsum('qap,kap->qkp', slip_amount, schmid_points, precision=lax.Precision.HIGHEST)
    stress = elastic(strain - plastic - increment)
    nodal = jnp.dot(derivative.T, stress.reshape(48, element_count), precision=lax.Precision.HIGHEST)
    return (quad_weight * nodal).reshape(3, 8, element_count)

def reference(history, child_octant, partition_offsets, connectivity, ghost_list, grain_id, schmid, displacement, step_size, load):
    capacity = 16 * PAR_DEV
    child_index = jnp.arange(CHILDREN, dtype=jnp.int32)
    holder = (jnp.searchsorted(partition_offsets, child_index, side='right') - 1).astype(jnp.int32)
    source_row = (holder * capacity + child_index - partition_offsets[holder]).astype(jnp.int32)
    child_rows = history[source_row].reshape(N_CURVE, PAR_DEV, 8, 8 * HIST)
    octant_list = child_octant[source_row].reshape(N_CURVE, PAR_DEV, 8)
    projector = jnp.asarray(projection_table(), jnp.float32)

    def project_block(pieces):
        block_rows, block_octants = pieces
        selector = (block_octants[:, :, None] == jnp.arange(8, dtype=jnp.int32)[None, None, :]).astype(jnp.float32)
        by_octant = jnp.einsum('gco,gcf->gof', selector, block_rows, precision=lax.Precision.HIGHEST)
        projected = jnp.einsum('qj,gjf->gqf', projector, by_octant.reshape(PAR_DEV, 64, HIST), precision=lax.Precision.HIGHEST)
        return projected.reshape(PAR_DEV, 8 * HIST)
    parent_history = lax.map(project_block, (child_rows, octant_list)).reshape(PARENTS, 8 * HIST)
    node_dev = PAR_DEV + 2 * GHOST
    lists = ghost_list.reshape(2, N_CURVE, GHOST)
    devices = jnp.arange(N_CURVE, dtype=jnp.int32)[:, None]
    owned = devices * node_dev + jnp.arange(node_dev, dtype=jnp.int32)[None, :]
    from_lower = jnp.where(devices >= 1, (devices - 1) * node_dev + jnp.roll(lists[1], 1, axis=0), NODES)
    from_upper = jnp.where(devices < N_CURVE - 1, (devices + 1) * node_dev + jnp.roll(lists[0], -1, axis=0), NODES)
    global_nodes = jnp.concatenate([owned, from_lower, from_upper], axis=1).astype(jnp.int32)
    blocks = connectivity.reshape(8, N_CURVE, PAR_DEV)
    corners = global_nodes[jnp.arange(N_CURVE, dtype=jnp.int32)[None, :, None], blocks].reshape(8, PARENTS)
    history_points = parent_history.reshape(PARENTS, 8, HIST).transpose(1, 2, 0)
    selector = (grain_id[None, :] == jnp.arange(GRAINS, dtype=jnp.int32)[:, None]).astype(jnp.float32)
    schmid_points = jnp.dot(schmid.T, selector, precision=lax.Precision.HIGHEST).reshape(6, SLIP, PARENTS)

    def residual_of(field):
        padded_octants = jnp.concatenate([field, jnp.zeros((3, 1), jnp.float32)], axis=1)
        nodal = forces(padded_octants[:, corners], history_points, schmid_points)
        assembled = jnp.zeros((3, NODES + 1), jnp.float32).at[:, corners].add(nodal)[:, :NODES]
        return assembled - load
    residual_first = residual_of(displacement)
    moved = displacement - step_size[None, :] * residual_first
    return (parent_history, residual_of(moved))
```

```python
import functools
import math

import jax
import jax.numpy as jnp
import ml_dtypes
import numpy as np
from jax import lax
from jax.experimental import pallas as pl
from jax.experimental.pallas import tpu as pltpu
from jax.sharding import PartitionSpec as P

SLIP = 48
ROOT3 = math.sqrt(3.0)
SLIP_RATE = 0.1
PAR = 512
CAP = 8192
BLOCK = 256
NCHUNK = CAP // BLOCK
FRONT = 256
ROWS = FRONT + CAP + BLOCK + 16
SIGNED = 18 * BLOCK
GH = 128
MSG = 264
F32 = jnp.float32
BF16 = jnp.bfloat16
VMEM = pl.BlockSpec(memory_space=pltpu.VMEM)
SMEM = pl.BlockSpec(memory_space=pltpu.SMEM)
HBM = pl.BlockSpec(memory_space=pl.ANY)


def strain_table():
    root_third = 1.0 / math.sqrt(3.0)
    table = np.zeros((48, 24))
    for quad_point in range(8):
        gauss_points = [
            (2 * (quad_point >> direction & 1) - 1) * root_third for direction in range(3)
        ]
        for corner in range(8):
            corner_signs = [2 * (corner >> direction & 1) - 1 for direction in range(3)]
            slopes = []
            for direction in range(3):
                factor = 0.25 * corner_signs[direction]
                for other_axis in range(3):
                    if other_axis != direction:
                        factor = factor * (
                            1.0 + corner_signs[other_axis] * gauss_points[other_axis]
                        )
                slopes.append(factor)
            row_base = quad_point * 6
            table[row_base + 0, corner] += slopes[0]
            table[row_base + 1, 8 + corner] += slopes[1]
            table[row_base + 2, 16 + corner] += slopes[2]
            table[row_base + 3, 8 + corner] += slopes[2]
            table[row_base + 3, 16 + corner] += slopes[1]
            table[row_base + 4, corner] += slopes[2]
            table[row_base + 4, 16 + corner] += slopes[0]
            table[row_base + 5, corner] += slopes[1]
            table[row_base + 5, 8 + corner] += slopes[0]
    return table


def split_table(table, depth):
    padded = np.zeros((table.shape[0], depth), np.float32)
    padded[:, : table.shape[1]] = table
    high = padded.astype(ml_dtypes.bfloat16)
    low = (padded - high.astype(np.float32)).astype(ml_dtypes.bfloat16)
    return np.concatenate([high, low, high], axis=1)


def tables():
    by_component = strain_table().reshape(8, 6, 24).transpose(1, 0, 2).reshape(48, 24)
    force = np.zeros((32, 48))
    force[:24] = 0.125 * by_component.T
    return split_table(by_component, 32), split_table(force, 48)


def high_low(value):
    high = value.astype(BF16)
    return high, (value - high.astype(F32)).astype(BF16)


def split_dot(table, value):
    high, low = high_low(value)
    return jnp.dot(table, jnp.concatenate([high, high, low], axis=0), preferred_element_type=F32)


def lane_take(row, index):
    return jnp.take_along_axis(row, index, axis=1, mode="promise_in_bounds")


def rows_of(row):
    return jnp.broadcast_to(row, (8, 128))


def sublanes():
    return lax.broadcasted_iota(jnp.int32, (8, 128), 0)


def pick_nodes(block, index):
    index = rows_of(index)
    taken = lane_take(block, index & 127)
    return jnp.sum(jnp.where(sublanes() == (index >> 7), taken, 0.0), axis=0, keepdims=True)


def project(first, last, place, begin, end, history_ref, out_ref, work, sems):
    buffers, signs, spread, ones, signed = work
    base_block = begin // BLOCK
    shift = begin - BLOCK * base_block
    count = end - begin
    low = first // 4 - base_block
    high = jnp.where(first < last, (last + 3) // 4 - base_block, low)
    chunks_end = jnp.minimum(high, (count + BLOCK - 1) // BLOCK)
    first_chunk = jnp.where(first < last, jnp.maximum(low - 1, 0), chunks_end)

    def copies(chunk):
        return [
            pltpu.make_async_copy(
                history_ref.at[
                    pl.ds(pl.multiple_of(chunk * BLOCK, BLOCK), BLOCK), pl.ds(128 * t, 128)
                ],
                buffers[t].at[pl.ds(pl.multiple_of(FRONT + chunk * BLOCK, BLOCK), BLOCK)],
                sems.at[t, chunk],
            )
            for t in range(4)
        ]

    def start():
        @pl.loop(first_chunk, chunks_end)
        def _(chunk):
            for copy in copies(chunk):
                copy.start()

    def wait(chunk):
        for copy in copies(chunk):
            copy.wait()

    def sign_row_of(block):
        return 8 + 2 * block - shift // 128

    def lay_signs():
        @pl.loop(0, (high - low + 1) // 2)
        def _(step):
            row = sign_row_of(low + 2 * step)
            tables = []
            for quarter in range(4):
                parts = []
                for direction in (1, 2):
                    sign = jnp.broadcast_to(
                        signs[direction][pl.ds(row + quarter, 1), :], (16, 128)
                    )
                    sign = jnp.concatenate([sign.astype(BF16)] * 8, axis=0)
                    parts.append(spread[...] * sign)
                tables.append(jnp.concatenate(parts, axis=1))
            laid = jnp.dot(
                jnp.concatenate(tables, axis=0), ones[...], preferred_element_type=F32
            )
            at = pl.ds(pl.multiple_of(2 * BLOCK * step, 2 * BLOCK), 2 * BLOCK)
            signed[at, :] = laid * ROOT3

    def compute(sent=None):
        lane = lax.broadcasted_iota(jnp.int32, (8, 128), 1)
        half_sign = jnp.where(lane < 64, -0.5 / 64.0, 0.5 / 64.0).astype(F32)
        index0 = sublanes() * 8

        @pl.when((first_chunk < low) & (first_chunk < chunks_end))
        def _():
            wait(first_chunk)

        @pl.loop(low, high)
        def _(block):
            @pl.when(block < chunks_end)
            def _():
                wait(block)

            @pl.when((block == high - 1) & (BLOCK * high - shift > count))
            def _():
                tail = 8 * (count // 8)
                for step in range(9):
                    at = pl.multiple_of(FRONT + tail + 8 * step, 8)
                    held = tail + 8 * step + sublanes() < count
                    for t in range(4):
                        buffers[t][pl.ds(at, 8), :] = jnp.where(
                            held, buffers[t][pl.ds(at, 8), :], 0.0
                        )

            row = sign_row_of(block)
            for i in range(4):
                base = BLOCK * block + 64 * i + FRONT - shift
                sign_row = rows_of(signs[0][pl.ds(row + i // 2, 1), :])
                acc = acc0 = None
                for c in range(8):
                    at = 128 * (i // 2) + 16 * c + 8 * (i % 2)
                    at = pl.ds(pl.multiple_of(BLOCK * (block - low) + at, 8), 8)
                    g0 = lane_take(sign_row, index0 + (c + 64 * (i % 2)))
                    g1 = signed[at, 0:128]
                    g2 = signed[at, 128:256]
                    v = [buffers[t][pl.ds(base + c, 8, stride=8), :] for t in range(4)]
                    s0, d0 = v[0] + v[1], v[1] - v[0]
                    s1, d1 = v[2] + v[3], v[3] - v[2]
                    d0 = d0 + g1 * s0
                    d1 = d1 + g1 * s1
                    ss, ds = s0 + s1, s1 - s0
                    sd, dd = d0 + d1, d1 - d0
                    ds = ds + g2 * ss
                    dd = dd + g2 * sd
                    y = [ss, sd, ds, dd]
                    y0 = [g0 * value for value in y]
                    acc = y if acc is None else [a + b for a, b in zip(acc, y)]
                    acc0 = y0 if acc0 is None else [a + b for a, b in zip(acc0, y0)]
                z = []
                for a, b in zip(acc, acc0):
                    b = half_sign * b
                    z.append((1.5 / 64.0) * a + b + pltpu.roll((0.5 / 64.0) * a - b, 64, 1))
                ss, sd, ds, dd = z
                ds, dd = 0.5 * ds, 0.5 * dd
                s0, s1 = ss - ds, ss + ds
                d0, d1 = 0.5 * (sd - dd), 0.5 * (sd + dd)
                outs = [s0 - d0, s0 + d0, s1 - d1, s1 + d1]
                at = pl.multiple_of(8 * (4 * (base_block + block) + i) + place, 8)
                for t in range(4):
                    out_ref[pl.ds(at, 8), 128 * t : 128 * t + 128] = outs[t]
            if sent is not None:
                sent(pl.multiple_of(32 * (base_block + block) + place, 32)).start()

        if sent is not None:

            @pl.loop(low, high)
            def _(block):
                sent(pl.multiple_of(32 * (base_block + block) + place, 32)).wait()

    return start, lay_signs, compute


def prepare_projection(begin, octant_ref, work, lagged):
    buffers, signs, spread, ones, _ = work
    shift = begin % 128
    for buffer in buffers:
        buffer[FRONT - 64 : FRONT, :] = jnp.zeros((64, 128), F32)
    lagged[8:72, :] = pltpu.roll(octant_ref[...], shift, 1)
    lagged[72:80, :] = jnp.zeros((8, 128), jnp.int32)
    lagged[0:8, :] = jnp.zeros((8, 128), jnp.int32)
    lane = lax.broadcasted_iota(jnp.int32, (72, 128), 1)
    octants = jnp.where(lane < shift, lagged[7:79, :], lagged[8:80, :])
    for direction in range(3):
        size = ROOT3 if direction == 0 else 1.0
        signs[direction][0:8, :] = jnp.zeros((8, 128), F32)
        signs[direction][80:88, :] = jnp.zeros((8, 128), F32)
        signs[direction][8:80, :] = jnp.where(
            ((octants >> direction) & 1) == 1, size, -size
        ).astype(F32)
    row = lax.broadcasted_iota(jnp.int32, (128, 128), 0)
    column = lax.broadcasted_iota(jnp.int32, (128, 128), 1)
    picked = (row % 16) * 8 + row // 16
    spread[...] = jnp.where(column == picked, 1.0, 0.0).astype(BF16)
    row = lax.broadcasted_iota(jnp.int32, (256, 256), 0)
    column = lax.broadcasted_iota(jnp.int32, (256, 256), 1)
    ones[...] = jnp.where((row < 128) == (column < 128), 1.0, 0.0).astype(BF16)


class Either:
    def __init__(self, condition, yes, no, sems):
        self.condition, self.yes, self.no, self.sems = condition, yes, no, sems

    def __call__(self, first, size=32):
        rows = pl.ds(first, size)
        sem = self.sems.at[first // 32]

        def both(act):
            pl.when(self.condition)(lambda: act(self.yes(rows, sem)))
            pl.when(jnp.logical_not(self.condition))(lambda: act(self.no(rows, sem)))

        return Act(both)


class Act:
    def __init__(self, both):
        self.both = both

    def start(self):
        self.both(lambda copy: copy.start())

    def wait(self):
        self.both(lambda copy: copy.wait())


def border_kernel(
    offsets,
    octant_ref,
    ghost,
    disp,
    step,
    load,
    history_ref,
    cross,
    pair,
    b0,
    b1,
    b2,
    b3,
    g0,
    g1,
    g2,
    spread,
    ones,
    signed,
    lagged,
    sems,
    messages,
    out_sems,
):
    d = lax.axis_index("curve")
    parity = d % 2
    down, up = messages.at[0], messages.at[1]
    begin, end = offsets[d], offsets[d + 1]
    own_first = 64 * d
    own_last = 64 * d + 64
    work = (b0, b1, b2, b3), (g0, g1, g2), spread, ones, signed
    start_low, signs_low, compute_low = project(
        begin // 64,
        jnp.maximum(own_first, begin // 64),
        256 - PAR * d,
        begin,
        end,
        history_ref,
        down,
        work,
        sems.at[0:4],
    )
    start_high, signs_high, compute_high = project(
        own_last,
        (end + 63) // 64,
        -PAR * (d + 1),
        begin,
        end,
        history_ref,
        up,
        work,
        sems.at[4:8],
    )
    start_low()
    start_high()
    prepare_projection(begin, octant_ref, work, lagged)
    blocks = []
    pad = jnp.zeros((2, 128), F32)
    for row in range(7):
        if row == 3:
            parts = [step[128 * b : 128 * b + 128].reshape(1, 128) for b in range(6)]
        else:
            source, at = (disp, row) if row < 3 else (load, row - 4)
            parts = [source[at : at + 1, 128 * b : 128 * b + 128] for b in range(6)]
        blocks.append(jnp.concatenate(parts + [pad], axis=0))
    for which, out in ((0, down), (1, up)):
        index = ghost[which : which + 1, :]
        for row in range(7):
            out[256 + row : 257 + row, 0:128] = pick_nodes(blocks[row], index)

    def sender(which):
        def to_cross(rows, sem):
            return pltpu.make_async_copy(messages.at[which, rows], cross.at[rows], sem)

        def to_pair(rows, sem):
            return pltpu.make_async_copy(messages.at[which, rows], pair.at[rows], sem)

        return Either(parity == which, to_cross, to_pair, out_sems.at[which])

    values = [sender(which) for which in range(2)]
    for value in values:
        value(256, 8).start()
    signs_low()
    compute_low(values[0])
    signs_high()
    compute_high(values[1])
    for value in values:
        value(256, 8).wait()


def own_kernel(
    offsets,
    octant_ref,
    conn,
    ghost,
    grain,
    schmid,
    history_ref,
    own,
    hot,
    inverse,
    points,
    b0,
    b1,
    b2,
    b3,
    g0,
    g1,
    g2,
    spread,
    ones,
    signed,
    lagged,
    sems,
):
    d = lax.axis_index("curve")
    begin, end = offsets[d], offsets[d + 1]
    work = (b0, b1, b2, b3), (g0, g1, g2), spread, ones, signed
    start, lay_signs, compute = project(
        jnp.maximum(64 * d, begin // 64),
        jnp.minimum(64 * d + 64, (end + 63) // 64),
        -PAR * d,
        begin,
        end,
        history_ref,
        own,
        work,
        sems,
    )
    start()
    prepare_projection(begin, octant_ref, work, lagged)
    lane_iota = lax.broadcasted_iota(jnp.int32, (128, PAR), 0)
    for n in range(8):
        lanes = jnp.broadcast_to(conn[n : n + 1, :] & 127, (128, PAR))
        hot[:, n * PAR : n * PAR + PAR] = jnp.where(lanes == lane_iota, 1.0, 0.0).astype(BF16)
    lists = jnp.concatenate([ghost[0:1, :], ghost[1:2, :]], axis=1)
    number = lax.broadcasted_iota(jnp.int32, (16, 2 * GH), 1) + 1
    block_row = lax.broadcasted_iota(jnp.int32, (16, 2 * GH), 0)
    left = jnp.where((lists >> 7) == block_row, number, 0).astype(F32).astype(BF16)
    right = jnp.where(
        (lists & 127) == lax.broadcasted_iota(jnp.int32, (128, 2 * GH), 0), 1.0, 0.0
    ).astype(BF16)
    found = lax.dot_general(left, right, (((1,), (1,)), ((), ())), preferred_element_type=F32)
    inverse[...] = found[0:8].astype(jnp.int32)
    high, low = high_low(schmid[...])
    grains = lax.broadcasted_iota(jnp.int32, (64, PAR), 0)
    select = jnp.where(grains == jnp.broadcast_to(grain[...], (64, PAR)), 1.0, 0.0).astype(BF16)
    contract = (((0,), (0,)), ((), ()))
    points[...] = lax.dot_general(
        jnp.concatenate([high, low], axis=0),
        jnp.concatenate([select, select], axis=0),
        contract,
        preferred_element_type=F32,
    )
    lay_signs()
    compute()


def elastic(strains):
    volume = strains[0] + strains[1] + strains[2]
    return [volume + 1.5 * e for e in strains[:3]] + [0.75 * e for e in strains[3:]]


def sweep(table, conn, decay, plastic, points, hot, strain_lhs, force_lhs, strain, stress, spread):
    columns = []
    for t in range(4):
        index = conn[:, 128 * t : 128 * t + 128]
        block, lane = index >> 7, index & 127
        masks = [block == b for b in range(1, 8)]
        column = []
        for c in range(3):
            value = lane_take(rows_of(table[8 * c : 8 * c + 1, :]), lane)
            for b in range(1, 8):
                row = rows_of(table[8 * c + b : 8 * c + b + 1, :])
                value = jnp.where(masks[b - 1], lane_take(row, lane), value)
            column.append(value)
        column.append(jnp.zeros((8, 128), F32))
        columns.append(jnp.concatenate(column, axis=0))
    strain[...] = split_dot(strain_lhs[...], jnp.concatenate(columns, axis=1))

    def tile(t, _):
        at = pl.ds(pl.multiple_of(128 * t, 128), 128)
        elastic_strain = [strain[8 * k : 8 * k + 8, at] - plastic[8 * k : 8 * k + 8, at] for k in range(6)]
        trial = elastic(elastic_strain)
        increment = [jnp.zeros((8, 128), F32)] * 6
        for a in range(SLIP):
            vector = [rows_of(points[SLIP * k + a : SLIP * k + a + 1, at]) for k in range(6)]
            products = [x * y for x, y in zip(trial, vector)]
            resolved = ((products[0] + products[1]) + (products[2] + products[3])) + (
                products[4] + products[5]
            )
            slip = jnp.tanh(resolved * decay[8 * a : 8 * a + 8, at])
            increment = [x + slip * y for x, y in zip(increment, vector)]
        result = elastic([x - SLIP_RATE * y for x, y in zip(elastic_strain, increment)])
        for k in range(6):
            stress[8 * k : 8 * k + 8, at] = result[k]
        return 0

    lax.fori_loop(0, 4, tile, 0)
    nodal = split_dot(force_lhs[...], stress[...])
    high = nodal.astype(BF16).astype(F32)
    low = nodal - high
    blocks = lax.broadcasted_iota(jnp.int32, (8, PAR), 0)
    for n in range(8):
        mask = jnp.broadcast_to(conn[n : n + 1, :] >> 7, (8, PAR)) == blocks
        pieces = []
        for c in range(3):
            for part in (high, low):
                row = jnp.broadcast_to(part[8 * c + n : 8 * c + n + 1, :], (8, PAR))
                pieces.append(jnp.where(mask, row, 0.0))
        spread[:, n * PAR : n * PAR + PAR] = jnp.concatenate(pieces, axis=0).astype(BF16)
    sums = lax.dot_general(
        spread[...], hot[...], (((1,), (1,)), ((), ())), preferred_element_type=F32
    )
    return [sums[16 * c : 16 * c + 8] + sums[16 * c + 8 : 16 * c + 16] for c in range(3)]


def send_nodes(parity, down, up, cross, pair):
    even = jnp.full((8, 128), parity, jnp.int32) == 0
    cross[...] = jnp.where(even, down, up)
    pair[0:8, :] = jnp.where(even, up, 0.0)
    pair[8:16, :] = jnp.where(even, 0.0, down)


def receive_nodes(parity, cross, pair):
    even = jnp.full((8, 128), parity, jnp.int32) == 0
    lower = jnp.where(even, cross[...], pair[0:8, :])
    upper = jnp.where(even, pair[8:16, :], cross[...])
    return lower, upper


def first_kernel(
    offsets,
    cross_in,
    pair_in,
    own,
    conn,
    ghost,
    disp,
    step,
    load,
    points,
    hot,
    strain_lhs,
    force_lhs,
    history_out,
    decay,
    plastic,
    nodes,
    partial,
    cross,
    pair,
    turned,
    strain,
    stress,
    spread,
    received,
    in_sems,
):
    d = lax.axis_index("curve")
    parity = d % 2
    from_lower, from_upper = received.at[0], received.at[1]
    ins = [
        pltpu.make_async_copy(cross_in, received.at[parity], in_sems.at[0]),
        pltpu.make_async_copy(pair_in, received.at[1 - parity], in_sems.at[1]),
    ]
    for copy in ins:
        copy.start()
    begin, end = offsets[d], offsets[d + 1]
    own_first, own_end = begin // 64 - 64 * d, (end + 63) // 64 - 64 * d
    lower_end = (begin + 63) // 64 - 64 * d
    upper_first = end // 64 - 64 * d

    for c in range(3):
        for b in range(6):
            at = slice(128 * b, 128 * b + 128)
            nodes[8 * c + b : 8 * c + b + 1, :] = disp[c : c + 1, at]
            nodes[32 + 8 * c + b : 33 + 8 * c + b, :] = load[c : c + 1, at]
            if c == 0:
                nodes[24 + b : 25 + b, :] = step[at].reshape(1, 128)
    for copy in ins:
        copy.wait()
    for b, source in ((6, from_lower), (7, from_upper)):
        for row in range(7):
            nodes[8 * row + b : 8 * row + b + 1, :] = source[256 + row : 257 + row, 0:128]

    def gather_history(tile, source, offset, valid):
        for i in range(16):
            g = 16 * tile + i
            at = pl.ds(pl.multiple_of(8 * g, 8), 8)
            there = pl.ds(pl.multiple_of(8 * g - offset, 8), 8)
            mine = (g >= own_first) & (g < own_end)
            history_out[at, :] = jnp.where(mine, own[at, :], 0.0) + jnp.where(
                valid(g), source[there, :], 0.0
            )

    def turn(tile, _):
        at = pl.ds(pl.multiple_of(128 * tile, 128), 128)

        @pl.when(tile < 2)
        def _():
            gather_history(tile, from_lower, 0, lambda g: g < lower_end)

        @pl.when(tile >= 2)
        def _():
            gather_history(tile, from_upper, 256, lambda g: g >= upper_first)

        for pair in range(4):
            lanes = slice(128 * pair, 128 * pair + 128)
            turned[lanes, :] = history_out[at, lanes].T
        for a in range(SLIP):
            decay[8 * a : 8 * a + 8, at] = jnp.exp(-turned[pl.ds(a, 8, stride=64), :])
        for k in range(6):
            plastic[8 * k : 8 * k + 8, at] = turned[pl.ds(SLIP + k, 8, stride=64), :]
        return 0

    lax.fori_loop(0, 4, turn, 0)
    sums = sweep(
        nodes, conn, decay, plastic, points, hot, strain_lhs, force_lhs, strain, stress, spread
    )
    messages = []
    for which in range(2):
        rows = [sums[c][6 + which : 7 + which, :] for c in range(3)]
        rows += [pick_nodes(sums[c], ghost[which : which + 1, :]) for c in range(3)]
        messages.append(jnp.concatenate(rows + [jnp.zeros((2, 128), F32)], axis=0))
    send_nodes(parity, messages[0], messages[1], cross, pair)
    for c in range(3):
        partial[8 * c : 8 * c + 8, :] = sums[c]


def add_shared(sums, inverse, lower, upper):
    lane = (inverse - 1) & 127
    from_lower = lane_take(rows_of(lower), lane)
    from_upper = lane_take(rows_of(upper), lane)
    shared = jnp.where(inverse > GH, from_upper, from_lower)
    return sums + jnp.where(inverse > 0, shared, 0.0)


def second_kernel(
    cross_in,
    pair_in,
    conn,
    inverse,
    nodes,
    partial,
    decay,
    plastic,
    points,
    hot,
    strain_lhs,
    force_lhs,
    second,
    cross,
    pair,
    table,
    strain,
    stress,
    spread,
):
    parity = lax.axis_index("curve") % 2
    from_lower, from_upper = receive_nodes(parity, cross_in, pair_in)
    row = sublanes()
    places = inverse[...]
    for c in range(3):
        total = add_shared(
            partial[8 * c : 8 * c + 8, :], places, from_lower[c : c + 1, :], from_upper[c : c + 1, :]
        )
        ghost_sums = jnp.where(
            row == 6, rows_of(from_lower[3 + c : 4 + c, :]), rows_of(from_upper[3 + c : 4 + c, :])
        )
        total = total + jnp.where(row >= 6, ghost_sums, 0.0)
        residual = total - nodes[32 + 8 * c : 40 + 8 * c, :]
        table[8 * c : 8 * c + 8, :] = nodes[8 * c : 8 * c + 8, :] - nodes[24:32, :] * residual
    sums = sweep(
        table, conn, decay, plastic, points, hot, strain_lhs, force_lhs, strain, stress, spread
    )
    pad = jnp.zeros((5, 128), F32)
    down, up = [
        jnp.concatenate([sums[c][b : b + 1, :] for c in range(3)] + [pad], axis=0) for b in (6, 7)
    ]
    send_nodes(parity, down, up, cross, pair)
    for c in range(3):
        second[8 * c : 8 * c + 8, :] = sums[c] - nodes[32 + 8 * c : 40 + 8 * c, :]


def last_kernel(cross_in, pair_in, inverse, second, residual):
    parity = lax.axis_index("curve") % 2
    from_lower, from_upper = receive_nodes(parity, cross_in, pair_in)
    places = inverse[...]
    for c in range(3):
        total = add_shared(
            second[8 * c : 8 * c + 8, :], places, from_lower[c : c + 1, :], from_upper[c : c + 1, :]
        )
        for b in range(6):
            residual[c : c + 1, 128 * b : 128 * b + 128] = total[b : b + 1, :]


def call(kernel, outs, ins, scratch=(), limit=None, places=None):
    return pl.pallas_call(
        kernel,
        out_shape=[jax.ShapeDtypeStruct(shape, kind) for shape, kind in outs],
        in_specs=list(ins),
        out_specs=[VMEM] * len(outs) if places is None else places,
        scratch_shapes=list(scratch),
        compiler_params=pltpu.CompilerParams(vmem_limit_bytes=limit),
    )


def swap(value, first):
    count = lax.axis_size("curve")
    pairs = [(i, i + 1) for i in range(first, count - 1, 2)]
    return lax.ppermute(value, "curve", pairs + [(j, i) for i, j in pairs])


def exchange_nodes(cross, pair):
    groups = [[i, i + 1] for i in range(0, lax.axis_size("curve"), 2)]
    return swap(cross, 1), lax.psum(pair, "curve", axis_index_groups=groups)


def local(
    history,
    child_octant,
    partition_offsets,
    connectivity,
    ghost_list,
    grain_id,
    schmid,
    displacement,
    step_size,
    load,
):
    octants = child_octant.reshape(CAP // 128, 128)
    step = step_size
    grain = grain_id.reshape(1, PAR)
    strain_lhs, force_lhs = (jnp.asarray(table) for table in tables())
    staging = [pltpu.VMEM((ROWS, 128), F32)] * 4
    staging += [pltpu.VMEM((88, 128), F32)] * 3
    staging += [pltpu.VMEM((128, 128), BF16), pltpu.VMEM((256, 256), BF16)]
    staging += [pltpu.VMEM((SIGNED, 256), F32), pltpu.VMEM((80, 128), jnp.int32)]
    megabyte = 1 << 20

    cross, pair = call(
        border_kernel,
        [((MSG, 512), F32)] * 2,
        [SMEM] + [VMEM] * 5 + [HBM],
        staging
        + [
            pltpu.SemaphoreType.DMA((8, NCHUNK)),
            pltpu.VMEM((2, MSG, 512), F32),
            pltpu.SemaphoreType.DMA((2, 9)),
        ],
        58 * megabyte,
        [HBM, HBM],
    )(partition_offsets, octants, ghost_list, displacement, step, load, history)
    cross, pair = swap(cross, 1), swap(pair, 0)
    own, hot, inverse, points = call(
        own_kernel,
        [((PAR, 512), F32), ((128, 8 * PAR), BF16), ((8, 128), jnp.int32), ((288, PAR), F32)],
        [SMEM] + [VMEM] * 5 + [HBM],
        staging + [pltpu.SemaphoreType.DMA((4, NCHUNK))],
        49 * megabyte,
    )(partition_offsets, octants, connectivity, ghost_list, grain, schmid, history)
    work = [
        pltpu.VMEM((48, PAR), F32),
        pltpu.VMEM((48, PAR), F32),
        pltpu.VMEM((48, 8 * PAR), BF16),
    ]
    small, double = ((8, 128), F32), ((16, 128), F32)
    parent_history, decay, plastic, nodes, partial, cross, pair = call(
        first_kernel,
        [
            ((PAR, 512), F32),
            ((8 * SLIP, PAR), F32),
            ((48, PAR), F32),
            ((56, 128), F32),
            ((24, 128), F32),
            small,
            double,
        ],
        [SMEM, HBM, HBM] + [VMEM] * 10,
        [pltpu.VMEM((512, 128), F32)]
        + work
        + [pltpu.VMEM((2, MSG, 512), F32), pltpu.SemaphoreType.DMA((2,))],
        24 * megabyte,
    )(
        partition_offsets,
        cross,
        pair,
        own,
        connectivity,
        ghost_list,
        displacement,
        step,
        load,
        points,
        hot,
        strain_lhs,
        force_lhs,
    )
    cross, pair = exchange_nodes(cross, pair)
    second, cross, pair = call(
        second_kernel,
        [((24, 128), F32), small, double],
        [VMEM] * 12,
        [pltpu.VMEM((24, 128), F32)] + work,
        24 * megabyte,
    )(
        cross,
        pair,
        connectivity,
        inverse,
        nodes,
        partial,
        decay,
        plastic,
        points,
        hot,
        strain_lhs,
        force_lhs,
    )
    cross, pair = exchange_nodes(cross, pair)
    (residual,) = call(last_kernel, [((3, 768), F32)], [VMEM] * 4)(
        cross, pair, inverse, second
    )
    return (parent_history, residual)


def solution(mesh):
    in_specs = (
        P("curve", None),
        P("curve"),
        P(),
        P(None, "curve"),
        P(None, "curve"),
        P("curve"),
        P(),
        P(None, "curve"),
        P("curve"),
        P(None, "curve"),
    )
    out_specs = (P("curve", None), P(None, "curve"))
    return jax.shard_map(local, mesh=mesh, in_specs=in_specs, out_specs=out_specs, check_vma=False)
```

```python
import functools
import math

import jax
import jax.numpy as jnp
import ml_dtypes
import numpy as np
from jax import lax
from jax.experimental import pallas as pl
from jax.experimental.pallas import tpu as pltpu
from jax.sharding import PartitionSpec as P

SLIP = 48
ROOT3 = math.sqrt(3.0)
SLIP_RATE = 0.1
PAR = 512
CAP = 8192
BLOCK = 256
RING = 8
FRONT = 256
ROWS = FRONT + CAP + BLOCK + 16
GH = 128
MSG = 264
F32 = jnp.float32
BF16 = jnp.bfloat16
VMEM = pl.BlockSpec(memory_space=pltpu.VMEM)
SMEM = pl.BlockSpec(memory_space=pltpu.SMEM)
HBM = pl.BlockSpec(memory_space=pl.ANY)


def strain_table():
    root_third = 1.0 / math.sqrt(3.0)
    table = np.zeros((48, 24))
    for quad_point in range(8):
        gauss_points = [
            (2 * (quad_point >> direction & 1) - 1) * root_third for direction in range(3)
        ]
        for corner in range(8):
            corner_signs = [2 * (corner >> direction & 1) - 1 for direction in range(3)]
            slopes = []
            for direction in range(3):
                factor = 0.25 * corner_signs[direction]
                for other_axis in range(3):
                    if other_axis != direction:
                        factor = factor * (
                            1.0 + corner_signs[other_axis] * gauss_points[other_axis]
                        )
                slopes.append(factor)
            row_base = quad_point * 6
            table[row_base + 0, corner] += slopes[0]
            table[row_base + 1, 8 + corner] += slopes[1]
            table[row_base + 2, 16 + corner] += slopes[2]
            table[row_base + 3, 8 + corner] += slopes[2]
            table[row_base + 3, 16 + corner] += slopes[1]
            table[row_base + 4, corner] += slopes[2]
            table[row_base + 4, 16 + corner] += slopes[0]
            table[row_base + 5, corner] += slopes[1]
            table[row_base + 5, 8 + corner] += slopes[0]
    return table


def split_table(table, depth):
    padded = np.zeros((table.shape[0], depth), np.float32)
    padded[:, : table.shape[1]] = table
    high = padded.astype(ml_dtypes.bfloat16)
    low = (padded - high.astype(np.float32)).astype(ml_dtypes.bfloat16)
    return np.concatenate([high, low, high], axis=1)


def tables():
    by_component = strain_table().reshape(8, 6, 24).transpose(1, 0, 2).reshape(48, 24)
    force = np.zeros((32, 48))
    force[:24] = 0.125 * by_component.T
    return split_table(by_component, 32), split_table(force, 48)


def high_low(value):
    high = value.astype(BF16)
    return high, (value - high.astype(F32)).astype(BF16)


def split_dot(table, value):
    high, low = high_low(value)
    return jnp.dot(table, jnp.concatenate([high, high, low], axis=0), preferred_element_type=F32)


def lane_take(row, index):
    return jnp.take_along_axis(row, index, axis=1, mode="promise_in_bounds")


def rows_of(row):
    return jnp.broadcast_to(row, (8, 128))


def sublanes():
    return lax.broadcasted_iota(jnp.int32, (8, 128), 0)


def pick_nodes(block, index):
    index = rows_of(index)
    taken = lane_take(block, index & 127)
    return jnp.sum(jnp.where(sublanes() == (index >> 7), taken, 0.0), axis=0, keepdims=True)


def project(first, last, place, begin, end, history_ref, out_ref, work, sems):
    buffers, codes, middle = work
    base_block = begin // BLOCK
    shift = begin - BLOCK * base_block
    count = end - begin
    low = first // 4 - base_block
    high = jnp.where(first < last, (last + 3) // 4 - base_block, low)
    chunks_end = jnp.minimum(high, (count + BLOCK - 1) // BLOCK)
    first_chunk = jnp.where(first < last, jnp.maximum(low - 1, 0), chunks_end)

    def copies(chunk):
        return [
            pltpu.make_async_copy(
                history_ref.at[
                    pl.ds(pl.multiple_of(chunk * BLOCK, BLOCK), BLOCK), pl.ds(128 * t, 128)
                ],
                buffers[t].at[pl.ds(pl.multiple_of(FRONT + chunk * BLOCK, BLOCK), BLOCK)],
                sems.at[chunk % RING],
            )
            for t in range(4)
        ]

    def start():
        @pl.loop(first_chunk, jnp.minimum(first_chunk + RING, chunks_end))
        def _(chunk):
            for copy in copies(chunk):
                copy.start()

    def wait(chunk):
        whole = buffers[0].at[pl.ds(0, 4 * BLOCK)]
        pltpu.make_async_copy(whole, whole, sems.at[chunk % RING]).wait()

        @pl.when(chunk + RING < chunks_end)
        def _():
            for copy in copies(chunk + RING):
                copy.start()

    def compute(sent=None):
        lane = lax.broadcasted_iota(jnp.int32, (8, 128), 1)
        half_sign = jnp.where(lane < 64, -0.5 / 64.0, 0.5 / 64.0).astype(F32)
        index0 = sublanes() * 8

        def row_of(block):
            return pl.multiple_of(32 * (base_block + block) + place, 32)

        def finish(block):
            z = []
            for t in range(4):
                lanes = slice(128 * t, 128 * t + 128)
                z.append(middle[0:32, lanes] + pltpu.roll(middle[32:64, lanes], 64, 1))
            ss, sd, ds, dd = z
            ds, dd = 0.5 * ds, 0.5 * dd
            s0, s1 = ss - ds, ss + ds
            d0, d1 = 0.5 * (sd - dd), 0.5 * (sd + dd)
            outs = [s0 - d0, s0 + d0, s1 - d1, s1 + d1]
            at = row_of(block)
            for t in range(4):
                out_ref[pl.ds(at, 32), 128 * t : 128 * t + 128] = outs[t]

        def send(block):
            if sent is not None:

                @pl.when(block >= low + 2)
                def _():
                    sent(row_of(block - 2)).wait()

                sent(row_of(block)).start()

        @pl.when((first_chunk < low) & (first_chunk < chunks_end))
        def _():
            wait(first_chunk)

        @pl.loop(low, high)
        def _(block):
            @pl.when(block < chunks_end)
            def _():
                wait(block)

            @pl.when((block == high - 1) & (BLOCK * high - shift > count))
            def _():
                tail = 8 * (count // 8)
                for step in range(9):
                    at = pl.multiple_of(FRONT + tail + 8 * step, 8)
                    held = tail + 8 * step + sublanes() < count
                    for t in range(4):
                        buffers[t][pl.ds(at, 8), :] = jnp.where(
                            held, buffers[t][pl.ds(at, 8), :], 0.0
                        )

            finish(jnp.maximum(block - 1, low))
            row = 8 + 2 * block - shift // 128
            for i in range(4):
                base = BLOCK * block + 64 * i + FRONT - shift
                code_row = rows_of(codes[pl.ds(row + i // 2, 1), :])
                acc = acc0 = None
                for c in range(8):
                    code = lane_take(code_row, index0 + (c + 64 * (i % 2)))
                    g0 = jnp.where((code & 1) == 1, ROOT3, -ROOT3)
                    g1 = jnp.where((code & 2) == 2, ROOT3, -ROOT3)
                    g2 = jnp.where(code >= 4, ROOT3, -ROOT3)
                    v = [buffers[t][pl.ds(base + c, 8, stride=8), :] for t in range(4)]
                    s0, d0 = v[0] + v[1], v[1] - v[0]
                    s1, d1 = v[2] + v[3], v[3] - v[2]
                    d0 = d0 + g1 * s0
                    d1 = d1 + g1 * s1
                    ss, ds = s0 + s1, s1 - s0
                    sd, dd = d0 + d1, d1 - d0
                    ds = ds + g2 * ss
                    dd = dd + g2 * sd
                    y = [ss, sd, ds, dd]
                    y0 = [g0 * value for value in y]
                    acc = y if acc is None else [a + b for a, b in zip(acc, y)]
                    acc0 = y0 if acc0 is None else [a + b for a, b in zip(acc0, y0)]
                for t in range(4):
                    b = half_sign * acc0[t]
                    middle[8 * i : 8 * i + 8, 128 * t : 128 * t + 128] = (1.5 / 64.0) * acc[t] + b
                    middle[32 + 8 * i : 40 + 8 * i, 128 * t : 128 * t + 128] = (
                        0.5 / 64.0
                    ) * acc[t] - b

            @pl.when(block > low)
            def _():
                send(block - 1)

        @pl.when(low < high)
        def _():
            finish(high - 1)
            send(high - 1)

        if sent is not None:

            @pl.loop(jnp.maximum(low, high - 2), high)
            def _(block):
                sent(row_of(block)).wait()

    return start, compute


def prepare_projection(begin, octant_ref, work, lagged):
    buffers, codes, _ = work
    shift = begin % 128
    for buffer in buffers:
        buffer[FRONT - 64 : FRONT, :] = jnp.zeros((64, 128), F32)
    lagged[0:8, :] = jnp.zeros((8, 128), jnp.int32)
    lagged[8:72, :] = pltpu.roll(octant_ref[...], shift, 1)
    lagged[72:80, :] = jnp.zeros((8, 128), jnp.int32)
    lane = lax.broadcasted_iota(jnp.int32, (72, 128), 1)
    codes[0:8, :] = jnp.zeros((8, 128), jnp.int32)
    codes[8:80, :] = jnp.where(lane < shift, lagged[7:79, :], lagged[8:80, :])


class Either:
    def __init__(self, condition, yes, no, sems):
        self.condition, self.yes, self.no, self.sems = condition, yes, no, sems

    def __call__(self, first, size=32):
        rows = pl.ds(first, size)
        sem = self.sems.at[2 if size == 8 else (first // 32) % 2]

        def both(act):
            pl.when(self.condition)(lambda: act(self.yes(rows, sem)))
            pl.when(jnp.logical_not(self.condition))(lambda: act(self.no(rows, sem)))

        return Act(both)


class Act:
    def __init__(self, both):
        self.both = both

    def start(self):
        self.both(lambda copy: copy.start())

    def wait(self):
        self.both(lambda copy: copy.wait())


def border_kernel(
    offsets,
    octant_ref,
    ghost,
    disp,
    step,
    load,
    history_ref,
    cross,
    pair,
    b0,
    b1,
    b2,
    b3,
    codes,
    middle,
    lagged,
    sems,
    messages,
    out_sems,
):
    d = lax.axis_index("curve")
    parity = d % 2
    down, up = messages.at[0], messages.at[1]
    begin, end = offsets[d], offsets[d + 1]
    own_first = 64 * d
    own_last = 64 * d + 64
    work = (b0, b1, b2, b3), codes, middle
    start_low, compute_low = project(
        begin // 64,
        jnp.maximum(own_first, begin // 64),
        256 - PAR * d,
        begin,
        end,
        history_ref,
        down,
        work,
        sems.at[0:RING],
    )
    start_high, compute_high = project(
        own_last,
        (end + 63) // 64,
        -PAR * (d + 1),
        begin,
        end,
        history_ref,
        up,
        work,
        sems.at[RING : 2 * RING],
    )
    start_low()
    start_high()
    prepare_projection(begin, octant_ref, work, lagged)
    blocks = []
    pad = jnp.zeros((2, 128), F32)
    for row in range(7):
        if row == 3:
            parts = [step[128 * b : 128 * b + 128].reshape(1, 128) for b in range(6)]
        else:
            source, at = (disp, row) if row < 3 else (load, row - 4)
            parts = [source[at : at + 1, 128 * b : 128 * b + 128] for b in range(6)]
        blocks.append(jnp.concatenate(parts + [pad], axis=0))
    for which, out in ((0, down), (1, up)):
        index = ghost[which : which + 1, :]
        for row in range(7):
            out[256 + row : 257 + row, 0:128] = pick_nodes(blocks[row], index)

    def sender(which):
        def to_cross(rows, sem):
            return pltpu.make_async_copy(messages.at[which, rows], cross.at[rows], sem)

        def to_pair(rows, sem):
            return pltpu.make_async_copy(messages.at[which, rows], pair.at[rows], sem)

        return Either(parity == which, to_cross, to_pair, out_sems.at[which])

    values = [sender(which) for which in range(2)]
    for value in values:
        value(256, 8).start()
    compute_low(values[0])
    compute_high(values[1])
    for value in values:
        value(256, 8).wait()


def own_kernel(
    offsets,
    octant_ref,
    conn,
    ghost,
    grain,
    schmid,
    history_ref,
    own,
    hot,
    inverse,
    points,
    b0,
    b1,
    b2,
    b3,
    codes,
    middle,
    lagged,
    sems,
):
    d = lax.axis_index("curve")
    begin, end = offsets[d], offsets[d + 1]
    work = (b0, b1, b2, b3), codes, middle
    start, compute = project(
        jnp.maximum(64 * d, begin // 64),
        jnp.minimum(64 * d + 64, (end + 63) // 64),
        -PAR * d,
        begin,
        end,
        history_ref,
        own,
        work,
        sems,
    )
    start()
    prepare_projection(begin, octant_ref, work, lagged)
    lane_iota = lax.broadcasted_iota(jnp.int32, (128, PAR), 0)
    for n in range(8):
        lanes = jnp.broadcast_to(conn[n : n + 1, :] & 127, (128, PAR))
        hot[:, n * PAR : n * PAR + PAR] = jnp.where(lanes == lane_iota, 1.0, 0.0).astype(BF16)
    lists = jnp.concatenate([ghost[0:1, :], ghost[1:2, :]], axis=1)
    number = lax.broadcasted_iota(jnp.int32, (16, 2 * GH), 1) + 1
    block_row = lax.broadcasted_iota(jnp.int32, (16, 2 * GH), 0)
    left = jnp.where((lists >> 7) == block_row, number, 0).astype(F32).astype(BF16)
    right = jnp.where(
        (lists & 127) == lax.broadcasted_iota(jnp.int32, (128, 2 * GH), 0), 1.0, 0.0
    ).astype(BF16)
    found = lax.dot_general(left, right, (((1,), (1,)), ((), ())), preferred_element_type=F32)
    inverse[...] = found[0:8].astype(jnp.int32)
    high, low = high_low(schmid[...])
    grains = lax.broadcasted_iota(jnp.int32, (64, PAR), 0)
    select = jnp.where(grains == jnp.broadcast_to(grain[...], (64, PAR)), 1.0, 0.0).astype(BF16)
    contract = (((0,), (0,)), ((), ()))
    points[...] = lax.dot_general(
        jnp.concatenate([high, low], axis=0),
        jnp.concatenate([select, select], axis=0),
        contract,
        preferred_element_type=F32,
    )
    compute()


def elastic(strains):
    volume = strains[0] + strains[1] + strains[2]
    return [volume + 1.5 * e for e in strains[:3]] + [0.75 * e for e in strains[3:]]


def sweep(table, conn, decay, plastic, points, hot, strain_lhs, force_lhs, strain, stress, spread):
    columns = []
    for t in range(4):
        index = conn[:, 128 * t : 128 * t + 128]
        block, lane = index >> 7, index & 127
        masks = [block == b for b in range(1, 8)]
        column = []
        for c in range(3):
            value = lane_take(rows_of(table[8 * c : 8 * c + 1, :]), lane)
            for b in range(1, 8):
                row = rows_of(table[8 * c + b : 8 * c + b + 1, :])
                value = jnp.where(masks[b - 1], lane_take(row, lane), value)
            column.append(value)
        column.append(jnp.zeros((8, 128), F32))
        columns.append(jnp.concatenate(column, axis=0))
    strain[...] = split_dot(strain_lhs[...], jnp.concatenate(columns, axis=1))

    def tile(t, _):
        at = pl.ds(pl.multiple_of(128 * t, 128), 128)
        elastic_strain = [strain[8 * k : 8 * k + 8, at] - plastic[8 * k : 8 * k + 8, at] for k in range(6)]
        trial = elastic(elastic_strain)
        increment = [jnp.zeros((8, 128), F32)] * 6
        for a in range(SLIP):
            vector = [rows_of(points[SLIP * k + a : SLIP * k + a + 1, at]) for k in range(6)]
            products = [x * y for x, y in zip(trial, vector)]
            resolved = ((products[0] + products[1]) + (products[2] + products[3])) + (
                products[4] + products[5]
            )
            slip = jnp.tanh(resolved * decay[8 * a : 8 * a + 8, at])
            increment = [x + slip * y for x, y in zip(increment, vector)]
        result = elastic([x - SLIP_RATE * y for x, y in zip(elastic_strain, increment)])
        for k in range(6):
            stress[8 * k : 8 * k + 8, at] = result[k]
        return 0

    lax.fori_loop(0, 4, tile, 0)
    nodal = split_dot(force_lhs[...], stress[...])
    high = nodal.astype(BF16).astype(F32)
    low = nodal - high
    blocks = lax.broadcasted_iota(jnp.int32, (8, PAR), 0)
    for n in range(8):
        mask = jnp.broadcast_to(conn[n : n + 1, :] >> 7, (8, PAR)) == blocks
        pieces = []
        for c in range(3):
            for part in (high, low):
                row = jnp.broadcast_to(part[8 * c + n : 8 * c + n + 1, :], (8, PAR))
                pieces.append(jnp.where(mask, row, 0.0))
        spread[:, n * PAR : n * PAR + PAR] = jnp.concatenate(pieces, axis=0).astype(BF16)
    sums = lax.dot_general(
        spread[...], hot[...], (((1,), (1,)), ((), ())), preferred_element_type=F32
    )
    return [sums[16 * c : 16 * c + 8] + sums[16 * c + 8 : 16 * c + 16] for c in range(3)]


def send_nodes(parity, down, up, cross, pair):
    even = jnp.full((8, 128), parity, jnp.int32) == 0
    cross[...] = jnp.where(even, down, up)
    pair[0:8, :] = jnp.where(even, up, 0.0)
    pair[8:16, :] = jnp.where(even, 0.0, down)


def receive_nodes(parity, cross, pair):
    even = jnp.full((8, 128), parity, jnp.int32) == 0
    lower = jnp.where(even, cross[...], pair[0:8, :])
    upper = jnp.where(even, pair[8:16, :], cross[...])
    return lower, upper


def first_kernel(
    offsets,
    cross_in,
    pair_in,
    own,
    conn,
    ghost,
    disp,
    step,
    load,
    points,
    hot,
    strain_lhs,
    force_lhs,
    history_out,
    decay,
    plastic,
    nodes,
    partial,
    cross,
    pair,
    turned,
    strain,
    stress,
    spread,
    received,
    in_sems,
):
    d = lax.axis_index("curve")
    parity = d % 2
    from_lower, from_upper = received.at[0], received.at[1]
    ins = [
        pltpu.make_async_copy(cross_in, received.at[parity], in_sems.at[0]),
        pltpu.make_async_copy(pair_in, received.at[1 - parity], in_sems.at[1]),
    ]
    for copy in ins:
        copy.start()
    begin, end = offsets[d], offsets[d + 1]
    own_first, own_end = begin // 64 - 64 * d, (end + 63) // 64 - 64 * d
    lower_end = (begin + 63) // 64 - 64 * d
    upper_first = end // 64 - 64 * d

    for c in range(3):
        for b in range(6):
            at = slice(128 * b, 128 * b + 128)
            nodes[8 * c + b : 8 * c + b + 1, :] = disp[c : c + 1, at]
            nodes[32 + 8 * c + b : 33 + 8 * c + b, :] = load[c : c + 1, at]
            if c == 0:
                nodes[24 + b : 25 + b, :] = step[at].reshape(1, 128)
    for copy in ins:
        copy.wait()
    for b, source in ((6, from_lower), (7, from_upper)):
        for row in range(7):
            nodes[8 * row + b : 8 * row + b + 1, :] = source[256 + row : 257 + row, 0:128]

    def gather_history(tile, source, offset, valid):
        for i in range(16):
            g = 16 * tile + i
            at = pl.ds(pl.multiple_of(8 * g, 8), 8)
            there = pl.ds(pl.multiple_of(8 * g - offset, 8), 8)
            mine = (g >= own_first) & (g < own_end)
            history_out[at, :] = jnp.where(mine, own[at, :], 0.0) + jnp.where(
                valid(g), source[there, :], 0.0
            )

    def turn(tile, _):
        at = pl.ds(pl.multiple_of(128 * tile, 128), 128)

        @pl.when(tile < 2)
        def _():
            gather_history(tile, from_lower, 0, lambda g: g < lower_end)

        @pl.when(tile >= 2)
        def _():
            gather_history(tile, from_upper, 256, lambda g: g >= upper_first)

        for pair in range(4):
            lanes = slice(128 * pair, 128 * pair + 128)
            turned[lanes, :] = history_out[at, lanes].T
        for a in range(SLIP):
            decay[8 * a : 8 * a + 8, at] = jnp.exp(-turned[pl.ds(a, 8, stride=64), :])
        for k in range(6):
            plastic[8 * k : 8 * k + 8, at] = turned[pl.ds(SLIP + k, 8, stride=64), :]
        return 0

    lax.fori_loop(0, 4, turn, 0)
    sums = sweep(
        nodes, conn, decay, plastic, points, hot, strain_lhs, force_lhs, strain, stress, spread
    )
    messages = []
    for which in range(2):
        rows = [sums[c][6 + which : 7 + which, :] for c in range(3)]
        rows += [pick_nodes(sums[c], ghost[which : which + 1, :]) for c in range(3)]
        messages.append(jnp.concatenate(rows + [jnp.zeros((2, 128), F32)], axis=0))
    send_nodes(parity, messages[0], messages[1], cross, pair)
    for c in range(3):
        partial[8 * c : 8 * c + 8, :] = sums[c]


def add_shared(sums, inverse, lower, upper):
    lane = (inverse - 1) & 127
    from_lower = lane_take(rows_of(lower), lane)
    from_upper = lane_take(rows_of(upper), lane)
    shared = jnp.where(inverse > GH, from_upper, from_lower)
    return sums + jnp.where(inverse > 0, shared, 0.0)


def second_kernel(
    cross_in,
    pair_in,
    conn,
    inverse,
    nodes,
    partial,
    decay,
    plastic,
    points,
    hot,
    strain_lhs,
    force_lhs,
    second,
    cross,
    pair,
    table,
    strain,
    stress,
    spread,
):
    parity = lax.axis_index("curve") % 2
    from_lower, from_upper = receive_nodes(parity, cross_in, pair_in)
    row = sublanes()
    places = inverse[...]
    for c in range(3):
        total = add_shared(
            partial[8 * c : 8 * c + 8, :], places, from_lower[c : c + 1, :], from_upper[c : c + 1, :]
        )
        ghost_sums = jnp.where(
            row == 6, rows_of(from_lower[3 + c : 4 + c, :]), rows_of(from_upper[3 + c : 4 + c, :])
        )
        total = total + jnp.where(row >= 6, ghost_sums, 0.0)
        residual = total - nodes[32 + 8 * c : 40 + 8 * c, :]
        table[8 * c : 8 * c + 8, :] = nodes[8 * c : 8 * c + 8, :] - nodes[24:32, :] * residual
    sums = sweep(
        table, conn, decay, plastic, points, hot, strain_lhs, force_lhs, strain, stress, spread
    )
    pad = jnp.zeros((5, 128), F32)
    down, up = [
        jnp.concatenate([sums[c][b : b + 1, :] for c in range(3)] + [pad], axis=0) for b in (6, 7)
    ]
    send_nodes(parity, down, up, cross, pair)
    for c in range(3):
        second[8 * c : 8 * c + 8, :] = sums[c] - nodes[32 + 8 * c : 40 + 8 * c, :]


def last_kernel(cross_in, pair_in, inverse, second, residual):
    parity = lax.axis_index("curve") % 2
    from_lower, from_upper = receive_nodes(parity, cross_in, pair_in)
    places = inverse[...]
    for c in range(3):
        total = add_shared(
            second[8 * c : 8 * c + 8, :], places, from_lower[c : c + 1, :], from_upper[c : c + 1, :]
        )
        for b in range(6):
            residual[c : c + 1, 128 * b : 128 * b + 128] = total[b : b + 1, :]


def call(kernel, outs, ins, scratch=(), limit=None, places=None):
    return pl.pallas_call(
        kernel,
        out_shape=[jax.ShapeDtypeStruct(shape, kind) for shape, kind in outs],
        in_specs=list(ins),
        out_specs=[VMEM] * len(outs) if places is None else places,
        scratch_shapes=list(scratch),
        compiler_params=pltpu.CompilerParams(vmem_limit_bytes=limit),
    )


def swap(value, first):
    count = lax.axis_size("curve")
    pairs = [(i, i + 1) for i in range(first, count - 1, 2)]
    return lax.ppermute(value, "curve", pairs + [(j, i) for i, j in pairs])


def exchange_nodes(cross, pair):
    groups = [[i, i + 1] for i in range(0, lax.axis_size("curve"), 2)]
    return swap(cross, 1), lax.psum(pair, "curve", axis_index_groups=groups)


def local(
    history,
    child_octant,
    partition_offsets,
    connectivity,
    ghost_list,
    grain_id,
    schmid,
    displacement,
    step_size,
    load,
):
    octants = child_octant.reshape(CAP // 128, 128)
    step = step_size
    grain = grain_id.reshape(1, PAR)
    strain_lhs, force_lhs = (jnp.asarray(table) for table in tables())
    staging = [pltpu.VMEM((ROWS, 128), F32)] * 4
    staging += [pltpu.VMEM((80, 128), jnp.int32), pltpu.VMEM((64, 512), F32)]
    staging += [pltpu.VMEM((80, 128), jnp.int32)]
    megabyte = 1 << 20

    cross, pair = call(
        border_kernel,
        [((MSG, 512), F32)] * 2,
        [SMEM] + [VMEM] * 5 + [HBM],
        staging
        + [
            pltpu.SemaphoreType.DMA((2 * RING,)),
            pltpu.VMEM((2, MSG, 512), F32),
            pltpu.SemaphoreType.DMA((2, 3)),
        ],
        58 * megabyte,
        [HBM, HBM],
    )(partition_offsets, octants, ghost_list, displacement, step, load, history)
    cross, pair = swap(cross, 1), swap(pair, 0)
    own, hot, inverse, points = call(
        own_kernel,
        [((PAR, 512), F32), ((128, 8 * PAR), BF16), ((8, 128), jnp.int32), ((288, PAR), F32)],
        [SMEM] + [VMEM] * 5 + [HBM],
        staging + [pltpu.SemaphoreType.DMA((RING,))],
        49 * megabyte,
    )(partition_offsets, octants, connectivity, ghost_list, grain, schmid, history)
    work = [
        pltpu.VMEM((48, PAR), F32),
        pltpu.VMEM((48, PAR), F32),
        pltpu.VMEM((48, 8 * PAR), BF16),
    ]
    small, double = ((8, 128), F32), ((16, 128), F32)
    parent_history, decay, plastic, nodes, partial, cross, pair = call(
        first_kernel,
        [
            ((PAR, 512), F32),
            ((8 * SLIP, PAR), F32),
            ((48, PAR), F32),
            ((56, 128), F32),
            ((24, 128), F32),
            small,
            double,
        ],
        [SMEM, HBM, HBM] + [VMEM] * 10,
        [pltpu.VMEM((512, 128), F32)]
        + work
        + [pltpu.VMEM((2, MSG, 512), F32), pltpu.SemaphoreType.DMA((2,))],
        24 * megabyte,
    )(
        partition_offsets,
        cross,
        pair,
        own,
        connectivity,
        ghost_list,
        displacement,
        step,
        load,
        points,
        hot,
        strain_lhs,
        force_lhs,
    )
    cross, pair = exchange_nodes(cross, pair)
    second, cross, pair = call(
        second_kernel,
        [((24, 128), F32), small, double],
        [VMEM] * 12,
        [pltpu.VMEM((24, 128), F32)] + work,
        24 * megabyte,
    )(
        cross,
        pair,
        connectivity,
        inverse,
        nodes,
        partial,
        decay,
        plastic,
        points,
        hot,
        strain_lhs,
        force_lhs,
    )
    cross, pair = exchange_nodes(cross, pair)
    (residual,) = call(last_kernel, [((3, 768), F32)], [VMEM] * 4, limit=24 * megabyte)(
        cross, pair, inverse, second
    )
    return (parent_history, residual)


def solution(mesh):
    in_specs = (
        P("curve", None),
        P("curve"),
        P(),
        P(None, "curve"),
        P(None, "curve"),
        P("curve"),
        P(),
        P(None, "curve"),
        P("curve"),
        P(None, "curve"),
    )
    out_specs = (P("curve", None), P(None, "curve"))
    return jax.shard_map(local, mesh=mesh, in_specs=in_specs, out_specs=out_specs, check_vma=False)
```
